32 devices in a mesh: groups: 2 (over y), tensor: 8 (over z, x), dp: 2 (over core).
Axes of the slice: x: 2, y: 2, z: 4, core: 2. Of those that a mesh axis runs over, the one named last changes fastest.
Arguments:
- layer_inputs: bfloat16 [16384, 8192], P(('groups', 'dp'), 'tensor'), parts along dimension 0, may hold values from -6 to 6
- output_grads: bfloat16 [16384, 28672], P(('groups', 'dp'), 'tensor'), parts along dimension 0, may hold values from -6 to 6
- proj_in: bfloat16 [8192, 64], P('tensor'), may hold values from -0.0625 to 0.0625
- proj_out: bfloat16 [28672, 64], P('tensor'), may hold values from -0.03125 to 0.03125
- inv_out: float32 [64, 64], replicated, may hold values from -0.3 to 4, as said below
- inv_in: float32 [64, 64], replicated, may hold values from -0.3 to 4, as said below
- stored: bfloat16 [2560, 4096], P(('groups', 'tensor', 'dp')), parts along dimension 0, may hold values from -0.01171875 to 0.01171875
- lengths: int32 [4, 64], P(('groups', 'dp')), parts along dimension 0, may hold values from 1 to 128, 4096 in all within a row
Outputs:
- scores: float32 [1280, 256], P(('tensor', 'dp'), 'groups'), parts along dimension 1
The draws below stay inside these ranges and needn't reach their ends.
There are 2 independent parts, one for each index of `groups`. The reference program is written for one: setup_inputs(seed, part) draws one part's arguments, and reference() takes and returns one part's arrays. A program takes and returns all parts, laid end to end along the dimension named above; an argument that names none is the same for every part. Nothing has to cross between parts.
Inputs may be any that keep to these rules, and one draw needn't show every extreme that they name: `lengths`: each row sums to 4096. `inv_out`: Symmetric. `inv_in`: Symmetric.
All inputs are finite; a program needn't handle non-finite values.
Results may differ from the reference program's by a relative error of at most 0.005.
Values may be sent and summed in bfloat16 or wider, within the bound.
A program may use at most 128 MiB of HBM per device.

```python
import math
import jax
import jax.numpy as jnp
import numpy as np
from jax import lax

D = 8192
FF = 28672
R = 64
LMAX = 128
TOK_DEV = 4096
EX_DEV = 64
TOKENS = 8192
EXAMPLES = 128
NTRAIN = 1280
N_DP = 2


def inverse_factor(key, spread, low, high):
    diag = jax.random.uniform(jax.random.fold_in(key, 1), (R,), jnp.float32, low, high)
    off = jax.random.normal(jax.random.fold_in(key, 2), (R, R), jnp.float32) * spread
    off = jnp.clip((off + off.T) * 0.5, -0.3, 0.3)
    eye = jnp.eye(R, dtype=jnp.float32)
    return off * (1.0 - eye) + eye * diag[None, :]


def draw_inv_out(key, part):
    key = jax.random.fold_in(key, 11)
    return inverse_factor(key, 0.0625, 0.5, 2.0)


def draw_inv_in(key, part):
    key = jax.random.fold_in(key, 12)
    return inverse_factor(key, 0.0625, 0.5, 2.0)


def steps_of(own_key, extent, split, least, high):
    factor_of = 1.0
    for dim, shards_of in split:
        draws = jax.random.uniform(jax.random.fold_in(jax.random.fold_in(own_key, 6), dim), (shards_of,), jnp.float32, least / len(split), high / len(split))
        factor_of = factor_of * jnp.repeat(jnp.exp(draws), extent[dim] // shards_of).reshape((-1,) + (1,) * (len(extent) - 1 - dim))
    return factor_of


def split_up(number_of, total, limit, lean):
    weights = [(1 << 20) // math.isqrt(standing ** lean) + 1 for standing in range(2, number_of + 1)]
    rest, given = total - limit - (number_of - 1), [1] * (number_of - 1)
    while rest > 0:
        candidates = [i for i in range(number_of - 1) if given[i] < limit]
        mass, budget = sum([weights[i] for i in candidates]), rest
        for i in candidates:
            more = min(limit - given[i], max(1, budget * weights[i] // mass), rest)
            given[i] = given[i] + more
            rest = rest - more
    return np.array([limit] + given)


def uneven_parts(stream_key, amount, total, most, lean):
    if amount == 2:
        one = jax.random.randint(stream_key, (), max(1, total - most), min(most, total - 1) + 1)
        return jnp.stack([one, total - one])
    sizes = jnp.asarray(split_up(amount, total, most, lean), jnp.int32)
    twos = (amount - 1) // 2
    donor, taker = sizes[1:1 + 2 * twos:2], sizes[2:2 + 2 * twos:2]
    slack = jnp.minimum(donor - 1, most - taker)
    moved = jax.random.randint(jax.random.fold_in(stream_key, 1), (twos,), 0, 1 << 20) % (slack + 1)
    sizes = sizes.at[1:1 + 2 * twos:2].set(donor - moved).at[2:2 + 2 * twos:2].set(taker + moved)
    return sizes[jax.random.permutation(jax.random.fold_in(stream_key, 2), amount)]


def centred(key, extent, scale, reach, split=(), held_as=jnp.bfloat16):
    array = jax.random.normal(key, extent, jnp.float32) * scale
    if len(split) > 0:
        array = steps_of(key, extent, split, -0.22, 0.18) * array
    return jnp.clip(array, min=-reach, max=reach).astype(held_as)


def setup_inputs(seed: int = 0, part: int = 0) -> dict:
    streams_of = jax.random.split(jax.random.key(seed), 9)
    part_splits = jax.random.split(jax.random.fold_in(streams_of[8], part), 9)
    layer_inputs = centred(part_splits[0], (TOKENS, D), 1.0, 6.0, ((0, 2), (1, 8)))
    output_grads = centred(part_splits[1], (TOKENS, FF), 1.0, 6.0, ((0, 2), (1, 8)))
    proj_in = centred(streams_of[2], (D, R), D ** -0.5, 0.0625, ((0, 8),))
    proj_out = centred(streams_of[3], (FF, R), FF ** -0.5, 0.03125, ((0, 8),))
    inv_out = draw_inv_out(jax.random.fold_in(streams_of[8], 71), part)
    inv_in = draw_inv_in(jax.random.fold_in(streams_of[8], 71), part)
    stored = centred(part_splits[6], (NTRAIN, R * R), (R * R * (TOK_DEV // EX_DEV)) ** -0.5, 0.01171875, ((0, 16),))
    lengths = jax.vmap(lambda own: uneven_parts(own, EX_DEV, TOK_DEV, LMAX, 1))(jax.random.split(part_splits[7], N_DP)).reshape((N_DP, EX_DEV)).astype(jnp.int32)
    return {"layer_inputs": layer_inputs, "output_grads": output_grads, "proj_in": proj_in, "proj_out": proj_out, "inv_out": inv_out, "inv_in": inv_in, "stored": stored, "lengths": lengths}


def reference(layer_inputs, output_grads, proj_in, proj_out, inv_out, inv_in, stored, lengths):
    xp = jnp.dot(layer_inputs, proj_in, preferred_element_type=jnp.float32).astype(jnp.bfloat16)
    gp = jnp.dot(output_grads, proj_out, preferred_element_type=jnp.float32).astype(jnp.bfloat16)
    flat = lengths.reshape(-1).astype(jnp.int32)
    ends = jnp.cumsum(flat).astype(jnp.int32)
    starts = (ends - flat).astype(jnp.int32)
    positions = jnp.arange(TOKENS, dtype=jnp.int32)

    def one_example(bounds):
        begin, finish = bounds
        member = ((positions >= begin) & (positions < finish)).astype(jnp.bfloat16)
        picked = gp * member[:, None]
        return jnp.dot(picked.T, xp, preferred_element_type=jnp.float32)

    sketch = lax.map(one_example, (starts, ends))
    query = jnp.einsum("ab,ebc,cd->ead", inv_out, sketch, inv_in, precision=lax.Precision.HIGHEST)
    query = query.astype(jnp.bfloat16).reshape(EXAMPLES, R * R)
    return jnp.dot(stored, query.T, preferred_element_type=jnp.float32)
```

```python
import functools
import jax
import jax.numpy as jnp
from jax import lax
from jax.experimental import pallas as pl
from jax.experimental.pallas import tpu as pltpu
from jax.sharding import PartitionSpec as P

MESH = pl.DeviceIdType.MESH
LONGEST = 128
WIRE_X = jnp.float32
WIRE_Z = jnp.float32
AHEAD = 3
LAG = 1


def window_of(total):
    return min(total, LONGEST + 16)


def inner_size(count):
    inner = 1
    while (2 * inner) ** 3 <= count:
        inner *= 2
    return inner


def token_kernel(
    outer, inner,
    x_hbm, g_hbm, w_in, w_out,
    tokens_out,
    x_buf, g_buf, w_x, w_g, own, send_x, recv_x, send_z, recv_z,
    tokens,
    load_sem, sx_sem, rx_sem, sz_sem, rz_sem, gz_send, gz_recv, gx_send, gx_recv,
):
    parts = outer * inner
    total = x_buf.shape[0]
    chunk = total // parts
    rank = w_in.shape[1]
    wide = 2 * rank
    me = lax.axis_index("tensor")
    my_o = me // inner
    my_i = me % inner

    def rows_of(o, i):
        return pl.ds(pl.multiple_of((o * inner + i) * chunk, chunk), chunk)

    order = []
    for s in range(outer):
        o = lax.rem(my_o + 1 + s, outer)
        for r in list(range(1, inner)) + [0]:
            order.append((s, r, o, lax.rem(my_i + r, inner)))

    def loads(k):
        _, _, o, i = order[k]
        rows = rows_of(o, i)
        return (
            pltpu.make_async_copy(x_hbm.at[rows], x_buf.at[rows], load_sem.at[0, k]),
            pltpu.make_async_copy(g_hbm.at[rows], g_buf.at[rows], load_sem.at[1, k]),
        )

    for k in range(min(AHEAD, parts)):
        for copy in loads(k):
            copy.start()

    barrier = pltpu.get_barrier_semaphore()
    peers = [{"tensor": lax.rem(my_o + s, outer) * inner + my_i} for s in range(1, outer)]
    peers += [{"tensor": my_o * inner + lax.rem(my_i + r, inner)} for r in range(1, inner)]
    for peer in peers:
        pl.semaphore_signal(barrier, inc=1, device_id=peer, device_id_type=MESH)

    w_x[...] = jnp.concatenate([w_in[...], jnp.zeros_like(w_in)], axis=1)
    w_g[...] = jnp.concatenate([jnp.zeros_like(w_out), w_out[...]], axis=1)
    pl.semaphore_wait(barrier, len(peers))

    sub = min(256, chunk)

    def project(k, dest):
        _, _, o, i = order[k]
        for copy in loads(k):
            copy.wait()
        if k + AHEAD < parts:
            for copy in loads(k + AHEAD):
                copy.start()
        base = (o * inner + i) * chunk

        @pl.loop(0, chunk // sub)
        def _(h):
            rows = pl.ds(pl.multiple_of(base + h * sub, sub), sub)
            value = jnp.dot(x_buf[rows, :], w_x[...], preferred_element_type=jnp.float32)
            value += jnp.dot(g_buf[rows, :], w_g[...], preferred_element_type=jnp.float32)
            dest[pl.ds(pl.multiple_of(h * sub, sub), sub), :] = value.astype(dest.dtype)

    def x_copy(s, r):
        return pltpu.make_async_remote_copy(
            src_ref=send_x.at[s, r - 1], dst_ref=recv_x.at[s, r - 1],
            send_sem=sx_sem.at[s, r - 1], recv_sem=rx_sem.at[s, r - 1],
            device_id={"tensor": my_o * inner + lax.rem(my_i + r, inner)}, device_id_type=MESH,
        )

    def z_copy(s):
        return pltpu.make_async_remote_copy(
            src_ref=send_z.at[s], dst_ref=recv_z.at[s],
            send_sem=sz_sem.at[s], recv_sem=rz_sem.at[s],
            device_id={"tensor": lax.rem(my_o + 1 + s, outer) * inner + my_i}, device_id_type=MESH,
        )

    def combine(s):
        value = own[s]
        for r in range(1, inner):
            x_copy(s, r).wait_recv()
            value = value + recv_x[s, r - 1].astype(jnp.float32)
        if s < outer - 1:
            send_z[s] = value.astype(send_z.dtype)
            z_copy(s).start()
        else:
            for q in range(outer - 1):
                z_copy(q).wait_recv()
                value = value + recv_z[q].astype(jnp.float32)
            tokens[rows_of(my_o, my_i), :] = value.astype(tokens.dtype)

    for k in range(parts):
        s, r, _, _ = order[k]
        if r:
            project(k, send_x.at[s, r - 1])
            x_copy(s, r).start()
        else:
            project(k, own.at[s])
            if s >= LAG:
                combine(s - LAG)
    for s in range(outer - min(LAG, outer), outer):
        combine(s)

    def gather_z(s):
        rows = rows_of(my_o, my_i)
        return pltpu.make_async_remote_copy(
            src_ref=tokens.at[rows], dst_ref=tokens.at[rows],
            send_sem=gz_send.at[s], recv_sem=gz_recv.at[s],
            device_id={"tensor": lax.rem(my_o + 1 + s, outer) * inner + my_i}, device_id_type=MESH,
        )

    def gather_x(s, r):
        rows = rows_of(lax.rem(my_o + outer - s, outer), my_i)
        return pltpu.make_async_remote_copy(
            src_ref=tokens.at[rows], dst_ref=tokens.at[rows],
            send_sem=gx_send.at[s, r - 1], recv_sem=gx_recv.at[s, r - 1],
            device_id={"tensor": my_o * inner + lax.rem(my_i + r, inner)}, device_id_type=MESH,
        )

    for s in range(outer - 1):
        gather_z(s).start()
    for r in range(1, inner):
        gather_x(0, r).start()
    for s in range(outer - 1):
        gather_z(s).wait_recv()
        for r in range(1, inner):
            gather_x(s + 1, r).start()
    for s in range(outer):
        for r in range(1, inner):
            gather_x(s, r).wait_recv()

    for s in range(outer):
        for r in range(1, inner):
            x_copy(s, r).wait_send()
            gather_x(s, r).wait_send()
    for s in range(outer - 1):
        z_copy(s).wait_send()
        gather_z(s).wait_send()
    tokens_out[...] = tokens[...]


def sketch_kernel(tokens, bounds, query, sketch):
    total, wide = tokens.shape
    rank = wide // 2
    examples = bounds.shape[1]
    window = window_of(total)
    row = lax.broadcasted_iota(jnp.int32, (window, wide), 0)
    left = lax.broadcasted_iota(jnp.int32, (window, wide), 1) < rank

    def example(e, carry):
        first = pl.multiple_of(bounds[0, e], 16)
        rows = tokens[pl.ds(first, window), :]
        wide_rows = rows.astype(jnp.float32)
        twice = jnp.where(left, wide_rows, pltpu.roll(wide_rows, rank, 1))
        inside = (row >= bounds[1, e]) & (row < bounds[2, e])
        picked = jnp.where(inside, twice, 0.0).astype(jnp.bfloat16)
        outer_product = lax.dot_general(
            rows, picked, (((0,), (0,)), ((), ())), preferred_element_type=jnp.float32
        )
        sketch[pl.ds(pl.multiple_of(e * rank, rank), rank), :] = outer_product[rank:, :]
        return carry

    lax.fori_loop(0, examples, example, 0, unroll=4)

    low = lax.broadcasted_iota(jnp.int32, (examples, wide), 1) < rank
    for a in range(0, rank, 2):
        pair = jnp.where(
            low,
            sketch[pl.ds(a, examples, stride=rank), :],
            sketch[pl.ds(a + 1, examples, stride=rank), :],
        )
        query[:, a * rank:(a + 2) * rank] = pair.astype(query.dtype)


def score_kernel(stored, query, out, both, pair_send, pair_recv):
    core = lax.axis_index("dp")
    examples = query.shape[0]
    barrier = pltpu.get_barrier_semaphore()
    pl.semaphore_signal(barrier, inc=1, device_id={"dp": 1 - core}, device_id_type=MESH)
    mine = pl.ds(pl.multiple_of(core * examples, examples), examples)
    both[mine, :] = query[...]
    pl.semaphore_wait(barrier, 1)
    swap = pltpu.make_async_remote_copy(
        src_ref=query, dst_ref=both.at[mine],
        send_sem=pair_send, recv_sem=pair_recv,
        device_id={"dp": 1 - core}, device_id_type=MESH,
    )
    swap.start()
    swap.wait()
    out[...] = lax.dot_general(
        stored[...], both[...], (((1,), (1,)), ((), ())), preferred_element_type=jnp.float32
    )


def on_device(parts, cores, layer_inputs, output_grads, proj_in, proj_out, inv_out, inv_in, stored, lengths):
    total, depth_in = layer_inputs.shape
    depth_out = output_grads.shape[1]
    rank = proj_in.shape[1]
    wide = 2 * rank
    inner = inner_size(parts)
    outer = parts // inner
    chunk = total // parts
    examples = lengths.shape[1]
    count = stored.shape[0]
    square = stored.astype(jnp.float32).reshape(count, rank, rank)
    moved = jnp.einsum("ac,jab,db->jcd", inv_out, square, inv_in, precision=lax.Precision.HIGHEST)
    moved = moved.reshape(count, rank * rank).astype(jnp.bfloat16)
    ends = jnp.cumsum(lengths[0])
    begins = ends - lengths[0]
    firsts = jnp.minimum((begins // 16) * 16, total - window_of(total))
    bounds = jnp.stack([firsts, begins - firsts, ends - firsts])
    vmem = pl.BlockSpec(memory_space=pltpu.VMEM)
    dma = pltpu.SemaphoreType.DMA
    tokens = pl.pallas_call(
        functools.partial(token_kernel, outer, inner),
        out_shape=jax.ShapeDtypeStruct((total, wide), jnp.bfloat16),
        in_specs=[pl.BlockSpec(memory_space=pl.ANY), pl.BlockSpec(memory_space=pl.ANY), vmem, vmem],
        out_specs=vmem,
        scratch_shapes=[
            pltpu.VMEM((total, depth_in), jnp.bfloat16),
            pltpu.VMEM((total, depth_out), jnp.bfloat16),
            pltpu.VMEM((depth_in, wide), jnp.bfloat16),
            pltpu.VMEM((depth_out, wide), jnp.bfloat16),
            pltpu.VMEM((outer, chunk, wide), jnp.float32),
            pltpu.VMEM((outer, inner - 1, chunk, wide), WIRE_X),
            pltpu.VMEM((outer, inner - 1, chunk, wide), WIRE_X),
            pltpu.VMEM((outer - 1, chunk, wide), WIRE_Z),
            pltpu.VMEM((outer - 1, chunk, wide), WIRE_Z),
            pltpu.VMEM((total, wide), jnp.bfloat16),
            dma((2, parts)),
            dma((outer, inner - 1)), dma((outer, inner - 1)),
            dma((outer - 1,)), dma((outer - 1,)),
            dma((outer - 1,)), dma((outer - 1,)),
            dma((outer, inner - 1)), dma((outer, inner - 1)),
        ],
        compiler_params=pltpu.CompilerParams(
            collective_id=0, has_side_effects=True, vmem_limit_bytes=58 * 1024 * 1024
        ),
    )(layer_inputs, output_grads, proj_in, proj_out)
    query = pl.pallas_call(
        sketch_kernel,
        out_shape=jax.ShapeDtypeStruct((examples, rank * rank), jnp.bfloat16),
        in_specs=[vmem, pl.BlockSpec(memory_space=pltpu.SMEM)],
        out_specs=vmem,
        scratch_shapes=[pltpu.VMEM((examples * rank, wide), jnp.float32)],
        compiler_params=pltpu.CompilerParams(vmem_limit_bytes=32 * 1024 * 1024),
    )(tokens, bounds)
    return pl.pallas_call(
        score_kernel,
        out_shape=jax.ShapeDtypeStruct((count, cores * examples), jnp.float32),
        in_specs=[vmem, vmem],
        out_specs=vmem,
        scratch_shapes=[pltpu.VMEM((cores * examples, rank * rank), jnp.bfloat16), dma, dma],
        compiler_params=pltpu.CompilerParams(
            collective_id=1, has_side_effects=True, vmem_limit_bytes=32 * 1024 * 1024
        ),
    )(moved, query)


def solution(mesh):
    placed = (
        P(("groups", "dp"), "tensor"),
        P(("groups", "dp"), "tensor"),
        P("tensor", None),
        P("tensor", None),
        P(),
        P(),
        P(("groups", "tensor", "dp"), None),
        P(("groups", "dp"), None),
    )
    return jax.shard_map(
        functools.partial(on_device, mesh.shape["tensor"], mesh.shape["dp"]),
        mesh=mesh,
        in_specs=placed,
        out_specs=P(("tensor", "dp"), "groups"),
        check_vma=False,
    )
```

```python
import functools
import jax
import jax.numpy as jnp
from jax import lax
from jax.experimental import pallas as pl
from jax.experimental.pallas import tpu as pltpu
from jax.sharding import PartitionSpec as P

MESH = pl.DeviceIdType.MESH
LONGEST = 128
WIRE_X = jnp.float32
WIRE_Z = jnp.float32
AHEAD = 3
LAG = 1


def window_of(total):
    return min(total, LONGEST + 16)


def inner_size(count):
    inner = 1
    while (2 * inner) ** 3 <= count:
        inner *= 2
    return inner


def across(left, right):
    return lax.dot_general(left, right, (((1,), (1,)), ((), ())), preferred_element_type=jnp.float32)


def split(value):
    high = value.astype(jnp.bfloat16)
    return high, (value - high.astype(jnp.float32)).astype(jnp.bfloat16)


def move_preconditioner(stored, inv_out, inv_in, mixed, moved):
    count = stored.shape[0]
    rank = inv_in.shape[0]
    wide = 2 * rank
    high, low = split(inv_in[...])
    high = jnp.concatenate([high, high], axis=1)
    low = jnp.concatenate([low, low], axis=1)
    none = jnp.zeros_like(high)
    first = jnp.concatenate([high, none, low, none], axis=0)
    second = jnp.concatenate([none, high, none, low], axis=0)
    for a in range(0, rank, 2):
        pair = stored[:, a * rank:(a + 2) * rank]
        pair = jnp.concatenate([pair, pair], axis=1)
        mixed[pl.ds(a, count, stride=rank), :] = jnp.dot(
            pair, first, preferred_element_type=jnp.float32
        )
        mixed[pl.ds(a + 1, count, stride=rank), :] = jnp.dot(
            pair, second, preferred_element_type=jnp.float32
        )
    out_high, out_low = split(inv_out[...])
    factor = jnp.concatenate([out_high, out_low, out_high], axis=1)

    def one(j, carry):
        rows = pl.ds(pl.multiple_of(j * rank, rank), rank)
        row_high, row_low = split(mixed[rows, :])
        mixed[rows, :] = jnp.dot(
            factor,
            jnp.concatenate([row_high, row_high, row_low], axis=0),
            preferred_element_type=jnp.float32,
        )
        return carry

    lax.fori_loop(0, count, one, 0, unroll=4)
    left = lax.broadcasted_iota(jnp.int32, (count, wide), 1) < rank
    for a in range(0, rank, 2):
        moved[:, a * rank:(a + 2) * rank] = jnp.where(
            left,
            mixed[pl.ds(a, count, stride=rank), :],
            mixed[pl.ds(a + 1, count, stride=rank), :],
        ).astype(moved.dtype)


def token_kernel(
    outer, inner,
    x_hbm, g_hbm, w_in, w_out, stored, inv_out, inv_in,
    tokens_out, moved_out,
    x_buf, g_buf, w_x, w_g, own, send_x, recv_x, send_z, recv_z,
    tokens, mixed,
    load_sem, sx_sem, rx_sem, sz_sem, rz_sem, gz_send, gz_recv, gx_send, gx_recv,
):
    parts = outer * inner
    total = x_buf.shape[0]
    chunk = total // parts
    rank = w_in.shape[0]
    wide = 2 * rank
    me = lax.axis_index("tensor")
    my_o = me // inner
    my_i = me % inner

    def rows_of(o, i):
        return pl.ds(pl.multiple_of((o * inner + i) * chunk, chunk), chunk)

    order = []
    for s in range(outer):
        o = lax.rem(my_o + 1 + s, outer)
        for r in list(range(1, inner)) + [0]:
            order.append((s, r, o, lax.rem(my_i + r, inner)))

    def loads(k):
        _, _, o, i = order[k]
        rows = rows_of(o, i)
        return (
            pltpu.make_async_copy(x_hbm.at[rows], x_buf.at[rows], load_sem.at[0, k]),
            pltpu.make_async_copy(g_hbm.at[rows], g_buf.at[rows], load_sem.at[1, k]),
        )

    for k in range(min(AHEAD, parts)):
        for copy in loads(k):
            copy.start()

    barrier = pltpu.get_barrier_semaphore()
    peers = [{"tensor": lax.rem(my_o + s, outer) * inner + my_i} for s in range(1, outer)]
    peers += [{"tensor": my_o * inner + lax.rem(my_i + r, inner)} for r in range(1, inner)]
    for peer in peers:
        pl.semaphore_signal(barrier, inc=1, device_id=peer, device_id_type=MESH)

    w_x[...] = jnp.concatenate([w_in[...], jnp.zeros_like(w_in)], axis=0)
    w_g[...] = jnp.concatenate([jnp.zeros_like(w_out), w_out[...]], axis=0)
    pl.semaphore_wait(barrier, len(peers))

    sub = min(256, chunk)

    def project(k, dest):
        _, _, o, i = order[k]
        for copy in loads(k):
            copy.wait()
        if k + AHEAD < parts:
            for copy in loads(k + AHEAD):
                copy.start()
        base = (o * inner + i) * chunk

        @pl.loop(0, chunk // sub)
        def _(h):
            rows = pl.ds(pl.multiple_of(base + h * sub, sub), sub)
            value = across(x_buf[rows, :], w_x[...])
            value += across(g_buf[rows, :], w_g[...])
            dest[pl.ds(pl.multiple_of(h * sub, sub), sub), :] = value.astype(dest.dtype)

    def x_copy(s, r):
        return pltpu.make_async_remote_copy(
            src_ref=send_x.at[s, r - 1], dst_ref=recv_x.at[s, r - 1],
            send_sem=sx_sem.at[s, r - 1], recv_sem=rx_sem.at[s, r - 1],
            device_id={"tensor": my_o * inner + lax.rem(my_i + r, inner)}, device_id_type=MESH,
        )

    def z_copy(s):
        return pltpu.make_async_remote_copy(
            src_ref=send_z.at[s], dst_ref=recv_z.at[s],
            send_sem=sz_sem.at[s], recv_sem=rz_sem.at[s],
            device_id={"tensor": lax.rem(my_o + 1 + s, outer) * inner + my_i}, device_id_type=MESH,
        )

    def combine(s):
        value = own[s]
        for r in range(1, inner):
            x_copy(s, r).wait_recv()
            value = value + recv_x[s, r - 1].astype(jnp.float32)
        if s < outer - 1:
            send_z[s] = value.astype(send_z.dtype)
            z_copy(s).start()
        else:
            for q in range(outer - 1):
                z_copy(q).wait_recv()
                value = value + recv_z[q].astype(jnp.float32)
            tokens[rows_of(my_o, my_i), :] = value.astype(tokens.dtype)

    for k in range(parts):
        s, r, _, _ = order[k]
        if r:
            project(k, send_x.at[s, r - 1])
            x_copy(s, r).start()
        else:
            project(k, own.at[s])
            if s >= LAG:
                combine(s - LAG)
    for s in range(outer - min(LAG, outer), outer):
        if s == outer - 1:
            move_preconditioner(stored, inv_out, inv_in, mixed, moved_out)
        combine(s)

    def gather_z(s):
        rows = rows_of(my_o, my_i)
        return pltpu.make_async_remote_copy(
            src_ref=tokens.at[rows], dst_ref=tokens.at[rows],
            send_sem=gz_send.at[s], recv_sem=gz_recv.at[s],
            device_id={"tensor": lax.rem(my_o + 1 + s, outer) * inner + my_i}, device_id_type=MESH,
        )

    def gather_x(s, r):
        rows = rows_of(lax.rem(my_o + outer - s, outer), my_i)
        return pltpu.make_async_remote_copy(
            src_ref=tokens.at[rows], dst_ref=tokens.at[rows],
            send_sem=gx_send.at[s, r - 1], recv_sem=gx_recv.at[s, r - 1],
            device_id={"tensor": my_o * inner + lax.rem(my_i + r, inner)}, device_id_type=MESH,
        )

    for s in range(outer - 1):
        gather_z(s).start()
    for r in range(1, inner):
        gather_x(0, r).start()
    for s in range(outer - 1):
        gather_z(s).wait_recv()
        for r in range(1, inner):
            gather_x(s + 1, r).start()
    for s in range(outer):
        for r in range(1, inner):
            gather_x(s, r).wait_recv()

    for s in range(outer):
        for r in range(1, inner):
            x_copy(s, r).wait_send()
            gather_x(s, r).wait_send()
    for s in range(outer - 1):
        z_copy(s).wait_send()
        gather_z(s).wait_send()
    tokens_out[...] = tokens[...]


def sketch_kernel(tokens, lengths, query, sketch):
    total, wide = tokens.shape
    rank = wide // 2
    examples = lengths.shape[1]
    window = window_of(total)
    row = lax.broadcasted_iota(jnp.int32, (window, wide), 0)
    left = lax.broadcasted_iota(jnp.int32, (window, wide), 1) < rank

    def example(e, begin):
        finish = begin + lengths[0, e]
        first = pl.multiple_of(jnp.minimum((begin // 16) * 16, total - window), 16)
        rows = tokens[pl.ds(first, window), :]
        wide_rows = rows.astype(jnp.float32)
        twice = jnp.where(left, wide_rows, pltpu.roll(wide_rows, rank, 1))
        inside = (row >= begin - first) & (row < finish - first)
        picked = jnp.where(inside, twice, 0.0).astype(jnp.bfloat16)
        outer_product = lax.dot_general(
            rows, picked, (((0,), (0,)), ((), ())), preferred_element_type=jnp.float32
        )
        sketch[pl.ds(pl.multiple_of(e * rank, rank), rank), :] = outer_product[rank:, :]
        return finish

    lax.fori_loop(0, examples, example, jnp.int32(0), unroll=8)

    low = lax.broadcasted_iota(jnp.int32, (examples, wide), 1) < rank
    for a in range(0, rank, 2):
        pair = jnp.where(
            low,
            sketch[pl.ds(a, examples, stride=rank), :],
            sketch[pl.ds(a + 1, examples, stride=rank), :],
        )
        query[:, a * rank:(a + 2) * rank] = pair.astype(query.dtype)


def score_kernel(stored, query, out, both, pair_send, pair_recv):
    core = lax.axis_index("dp")
    examples = query.shape[0]
    barrier = pltpu.get_barrier_semaphore()
    pl.semaphore_signal(barrier, inc=1, device_id={"dp": 1 - core}, device_id_type=MESH)
    mine = pl.ds(pl.multiple_of(core * examples, examples), examples)
    both[mine, :] = query[...]
    pl.semaphore_wait(barrier, 1)
    swap = pltpu.make_async_remote_copy(
        src_ref=query, dst_ref=both.at[mine],
        send_sem=pair_send, recv_sem=pair_recv,
        device_id={"dp": 1 - core}, device_id_type=MESH,
    )
    swap.start()
    swap.wait()
    out[...] = lax.dot_general(
        stored[...], both[...], (((1,), (1,)), ((), ())), preferred_element_type=jnp.float32
    )


def on_device(parts, cores, layer_inputs, output_grads, proj_in, proj_out, inv_out, inv_in, stored, lengths):
    total, depth_in = layer_inputs.shape
    depth_out = output_grads.shape[1]
    rank = proj_in.shape[1]
    wide = 2 * rank
    inner = inner_size(parts)
    outer = parts // inner
    chunk = total // parts
    examples = lengths.shape[1]
    count = stored.shape[0]
    vmem = pl.BlockSpec(memory_space=pltpu.VMEM)
    dma = pltpu.SemaphoreType.DMA
    tokens, moved = pl.pallas_call(
        functools.partial(token_kernel, outer, inner),
        out_shape=(
            jax.ShapeDtypeStruct((total, wide), jnp.bfloat16),
            jax.ShapeDtypeStruct((count, rank * rank), jnp.bfloat16),
        ),
        in_specs=[pl.BlockSpec(memory_space=pl.ANY), pl.BlockSpec(memory_space=pl.ANY)] + [vmem] * 5,
        out_specs=(vmem, vmem),
        scratch_shapes=[
            pltpu.VMEM((total, depth_in), jnp.bfloat16),
            pltpu.VMEM((total, depth_out), jnp.bfloat16),
            pltpu.VMEM((wide, depth_in), jnp.bfloat16),
            pltpu.VMEM((wide, depth_out), jnp.bfloat16),
            pltpu.VMEM((outer, chunk, wide), jnp.float32),
            pltpu.VMEM((outer, inner - 1, chunk, wide), WIRE_X),
            pltpu.VMEM((outer, inner - 1, chunk, wide), WIRE_X),
            pltpu.VMEM((outer - 1, chunk, wide), WIRE_Z),
            pltpu.VMEM((outer - 1, chunk, wide), WIRE_Z),
            pltpu.VMEM((total, wide), jnp.bfloat16),
            pltpu.VMEM((count * rank, wide), jnp.float32),
            dma((2, parts)),
            dma((outer, inner - 1)), dma((outer, inner - 1)),
            dma((outer - 1,)), dma((outer - 1,)),
            dma((outer - 1,)), dma((outer - 1,)),
            dma((outer, inner - 1)), dma((outer, inner - 1)),
        ],
        compiler_params=pltpu.CompilerParams(
            collective_id=0, has_side_effects=True, vmem_limit_bytes=58 * 1024 * 1024
        ),
    )(layer_inputs, output_grads, proj_in.T, proj_out.T, stored, inv_out, inv_in)
    query = pl.pallas_call(
        sketch_kernel,
        out_shape=jax.ShapeDtypeStruct((examples, rank * rank), jnp.bfloat16),
        in_specs=[vmem, pl.BlockSpec(memory_space=pltpu.SMEM)],
        out_specs=vmem,
        scratch_shapes=[pltpu.VMEM((examples * rank, wide), jnp.float32)],
        compiler_params=pltpu.CompilerParams(vmem_limit_bytes=32 * 1024 * 1024),
    )(tokens, lengths)
    return pl.pallas_call(
        score_kernel,
        out_shape=jax.ShapeDtypeStruct((count, cores * examples), jnp.float32),
        in_specs=[vmem, vmem],
        out_specs=vmem,
        scratch_shapes=[pltpu.VMEM((cores * examples, rank * rank), jnp.bfloat16), dma, dma],
        compiler_params=pltpu.CompilerParams(
            collective_id=1, has_side_effects=True, vmem_limit_bytes=32 * 1024 * 1024
        ),
    )(moved, query)


def solution(mesh):
    placed = (
        P(("groups", "dp"), "tensor"),
        P(("groups", "dp"), "tensor"),
        P("tensor", None),
        P("tensor", None),
        P(),
        P(),
        P(("groups", "tensor", "dp"), None),
        P(("groups", "dp"), None),
    )
    return jax.shard_map(
        functools.partial(on_device, mesh.shape["tensor"], mesh.shape["dp"]),
        mesh=mesh,
        in_specs=placed,
        out_specs=P(("tensor", "dp"), "groups"),
        check_vma=False,
    )
```

```python
import functools
import jax
import jax.numpy as jnp
from jax import lax
from jax.experimental import pallas as pl
from jax.experimental.pallas import tpu as pltpu
from jax.sharding import PartitionSpec as P

MESH = pl.DeviceIdType.MESH
LONGEST = 128
AHEAD = 3
LAG = 1


def window_of(total):
    return min(total, LONGEST + 16)


def inner_size(count):
    inner = 1
    while (2 * inner) ** 3 <= count:
        inner *= 2
    return inner


def flip(place, bits):
    result, bit = place, 1
    while bit <= bits:
        if bits & bit:
            result = result + bit - 2 * bit * ((place // bit) % 2)
        bit *= 2
    return result


def across(left, right):
    return lax.dot_general(left, right, (((1,), (1,)), ((), ())), preferred_element_type=jnp.float32)


def split(value):
    high = value.astype(jnp.bfloat16)
    return high, (value - high.astype(jnp.float32)).astype(jnp.bfloat16)


def move_preconditioner(stored, inv_out, inv_in, mixed, moved):
    count = stored.shape[0]
    rank = inv_in.shape[0]
    wide = 2 * rank
    high, low = split(inv_in[...])
    high = jnp.concatenate([high, high], axis=1)
    low = jnp.concatenate([low, low], axis=1)
    none = jnp.zeros_like(high)
    first = jnp.concatenate([high, none, low, none], axis=0)
    second = jnp.concatenate([none, high, none, low], axis=0)
    for a in range(0, rank, 2):
        pair = stored[:, a * rank:(a + 2) * rank]
        pair = jnp.concatenate([pair, pair], axis=1)
        mixed[pl.ds(a, count, stride=rank), :] = jnp.dot(
            pair, first, preferred_element_type=jnp.float32
        )
        mixed[pl.ds(a + 1, count, stride=rank), :] = jnp.dot(
            pair, second, preferred_element_type=jnp.float32
        )
    out_high, out_low = split(inv_out[...])
    factor = jnp.concatenate([out_high, out_low, out_high], axis=1)

    def one(j, carry):
        rows = pl.ds(pl.multiple_of(j * rank, rank), rank)
        row_high, row_low = split(mixed[rows, :])
        mixed[rows, :] = jnp.dot(
            factor,
            jnp.concatenate([row_high, row_high, row_low], axis=0),
            preferred_element_type=jnp.float32,
        )
        return carry

    lax.fori_loop(0, count, one, 0, unroll=4)
    left = lax.broadcasted_iota(jnp.int32, (count, wide), 1) < rank
    for a in range(0, rank, 2):
        pair = jnp.where(
            left,
            mixed[pl.ds(a, count, stride=rank), :],
            mixed[pl.ds(a + 1, count, stride=rank), :],
        )
        moved[:count, a * rank:(a + 2) * rank], moved[count:, a * rank:(a + 2) * rank] = split(pair)


def token_kernel(
    outer, inner,
    x_hbm, g_hbm, w_in, w_out, stored, inv_out, inv_in,
    tokens_out, moved_out,
    x_buf, g_buf, w_x, w_g, own, send_x, recv_x, send_far, recv_far, send_near, recv_near,
    tokens, mixed,
    load_sem, sx_sem, rx_sem, sz_sem, rz_sem, gz_send, gz_recv, gx_send, gx_recv,
):
    parts = outer * inner
    total = x_buf.shape[0]
    chunk = total // parts
    rank = w_in.shape[0]
    wide = 2 * rank
    me = lax.axis_index("tensor")
    my_o = me // inner
    my_i = me % inner

    def rows_of(o, i):
        return pl.ds(pl.multiple_of((o * inner + i) * chunk, chunk), chunk)

    order = []
    for s in range(outer):
        o = flip(my_o, outer - 1 - s)
        for r in list(range(1, inner)) + [0]:
            order.append((s, r, o, lax.rem(my_i + r, inner)))

    def loads(k):
        _, _, o, i = order[k]
        rows = rows_of(o, i)
        return (
            pltpu.make_async_copy(x_hbm.at[rows], x_buf.at[rows], load_sem.at[0, k]),
            pltpu.make_async_copy(g_hbm.at[rows], g_buf.at[rows], load_sem.at[1, k]),
        )

    for k in range(min(AHEAD, parts)):
        for copy in loads(k):
            copy.start()

    barrier = pltpu.get_barrier_semaphore()
    peers = [{"tensor": flip(my_o, s) * inner + my_i} for s in range(1, outer)]
    peers += [{"tensor": my_o * inner + lax.rem(my_i + r, inner)} for r in range(1, inner)]
    for peer in peers:
        pl.semaphore_signal(barrier, inc=1, device_id=peer, device_id_type=MESH)

    w_x[...] = jnp.concatenate([w_in[...], jnp.zeros_like(w_in)], axis=0)
    w_g[...] = jnp.concatenate([jnp.zeros_like(w_out), w_out[...]], axis=0)
    pl.semaphore_wait(barrier, len(peers))

    sub = min(256, chunk)

    def project(k, dest):
        _, _, o, i = order[k]
        for copy in loads(k):
            copy.wait()
        if k + AHEAD < parts:
            for copy in loads(k + AHEAD):
                copy.start()
        base = (o * inner + i) * chunk

        @pl.loop(0, chunk // sub)
        def _(h):
            rows = pl.ds(pl.multiple_of(base + h * sub, sub), sub)
            value = across(x_buf[rows, :], w_x[...])
            value += across(g_buf[rows, :], w_g[...])
            dest[pl.ds(pl.multiple_of(h * sub, sub), sub), :] = value.astype(dest.dtype)

    def x_copy(s, r):
        return pltpu.make_async_remote_copy(
            src_ref=send_x.at[s, r - 1], dst_ref=recv_x.at[s, r - 1],
            send_sem=sx_sem.at[s, r - 1], recv_sem=rx_sem.at[s, r - 1],
            device_id={"tensor": my_o * inner + lax.rem(my_i + r, inner)}, device_id_type=MESH,
        )

    def send_z(s):
        return send_near if s == outer - 2 else send_far.at[s]

    def recv_z(s):
        return recv_near if s == outer - 2 else recv_far.at[s]

    def z_copy(s):
        return pltpu.make_async_remote_copy(
            src_ref=send_z(s), dst_ref=recv_z(s),
            send_sem=sz_sem.at[s], recv_sem=rz_sem.at[s],
            device_id={"tensor": flip(my_o, outer - 1 - s) * inner + my_i}, device_id_type=MESH,
        )

    def combine(s):
        value = own[s]
        for r in range(1, inner):
            x_copy(s, r).wait_recv()
            value = value + recv_x[s, r - 1].astype(jnp.float32)
        if s < outer - 1:
            target = send_z(s)
            target[...] = value.astype(target.dtype)
            z_copy(s).start()
        else:
            for q in range(outer - 1):
                z_copy(q).wait_recv()
                value = value + recv_z(q)[...].astype(jnp.float32)
            tokens[rows_of(my_o, my_i), :] = value.astype(tokens.dtype)

    for k in range(parts):
        s, r, _, _ = order[k]
        if r:
            project(k, send_x.at[s, r - 1])
            x_copy(s, r).start()
        else:
            project(k, own.at[s])
            if s >= LAG:
                combine(s - LAG)
    for s in range(outer - min(LAG, outer), outer):
        if s == outer - 1:
            move_preconditioner(stored, inv_out, inv_in, mixed, moved_out)
        combine(s)

    def gather_z(s):
        rows = rows_of(my_o, my_i)
        return pltpu.make_async_remote_copy(
            src_ref=tokens.at[rows], dst_ref=tokens.at[rows],
            send_sem=gz_send.at[s], recv_sem=gz_recv.at[s],
            device_id={"tensor": flip(my_o, outer - 1 - s) * inner + my_i}, device_id_type=MESH,
        )

    def gather_x(s, r):
        rows = rows_of(flip(my_o, outer - s) if s else my_o, my_i)
        return pltpu.make_async_remote_copy(
            src_ref=tokens.at[rows], dst_ref=tokens.at[rows],
            send_sem=gx_send.at[s, r - 1], recv_sem=gx_recv.at[s, r - 1],
            device_id={"tensor": my_o * inner + lax.rem(my_i + r, inner)}, device_id_type=MESH,
        )

    for s in range(outer - 1):
        gather_z(s).start()
    for r in range(1, inner):
        gather_x(0, r).start()
    for s in range(outer - 1):
        gather_z(s).wait_recv()
        for r in range(1, inner):
            gather_x(s + 1, r).start()
    for s in range(outer):
        for r in range(1, inner):
            gather_x(s, r).wait_recv()

    for s in range(outer):
        for r in range(1, inner):
            x_copy(s, r).wait_send()
            gather_x(s, r).wait_send()
    for s in range(outer - 1):
        z_copy(s).wait_send()
        gather_z(s).wait_send()
    tokens_out[...] = tokens[...]


def sketch_kernel(tokens, lengths, query, sketch):
    total, wide = tokens.shape
    rank = wide // 2
    examples = lengths.shape[1]
    window = window_of(total)
    row = lax.broadcasted_iota(jnp.int32, (window, wide), 0)
    left = lax.broadcasted_iota(jnp.int32, (window, wide), 1) < rank

    def example(e, begin):
        finish = begin + lengths[0, e]
        first = pl.multiple_of(jnp.minimum((begin // 16) * 16, total - window), 16)
        rows = tokens[pl.ds(first, window), :]
        wide_rows = rows.astype(jnp.float32)
        twice = jnp.where(left, wide_rows, pltpu.roll(wide_rows, rank, 1))
        inside = (row >= begin - first) & (row < finish - first)
        picked = jnp.where(inside, twice, 0.0).astype(jnp.bfloat16)
        outer_product = lax.dot_general(
            rows, picked, (((0,), (0,)), ((), ())), preferred_element_type=jnp.float32
        )
        sketch[pl.ds(pl.multiple_of(e * rank, rank), rank), :] = outer_product[rank:, :]
        return finish

    lax.fori_loop(0, examples, example, jnp.int32(0), unroll=8)

    low = lax.broadcasted_iota(jnp.int32, (examples, wide), 1) < rank
    for a in range(0, rank, 2):
        pair = jnp.where(
            low,
            sketch[pl.ds(a, examples, stride=rank), :],
            sketch[pl.ds(a + 1, examples, stride=rank), :],
        )
        columns = slice(a * rank, (a + 2) * rank)
        query[:examples, columns], query[examples:, columns] = split(pair)


def score_kernel(stored, query, out, both, pair_send, pair_recv):
    core = lax.axis_index("dp")
    examples = query.shape[0] // 2
    count = stored.shape[0] // 2
    barrier = pltpu.get_barrier_semaphore()
    pl.semaphore_signal(barrier, inc=1, device_id={"dp": 1 - core}, device_id_type=MESH)
    mine = pl.ds(pl.multiple_of(core * 2 * examples, 2 * examples), 2 * examples)
    both[mine, :] = query[...]
    pl.semaphore_wait(barrier, 1)
    swap = pltpu.make_async_remote_copy(
        src_ref=query, dst_ref=both.at[mine],
        send_sem=pair_send, recv_sem=pair_recv,
        device_id={"dp": 1 - core}, device_id_type=MESH,
    )
    swap.start()
    swap.wait()
    product = across(stored[...], both[...])
    halves = []
    for other in range(both.shape[0] // (2 * examples)):
        at = other * 2 * examples
        high = product[:, at:at + examples]
        halves.append(high[:count] + high[count:] + product[:count, at + examples:at + 2 * examples])
    out[...] = jnp.concatenate(halves, axis=1)


def on_device(parts, cores, layer_inputs, output_grads, proj_in, proj_out, inv_out, inv_in, stored, lengths):
    total, depth_in = layer_inputs.shape
    depth_out = output_grads.shape[1]
    rank = proj_in.shape[1]
    wide = 2 * rank
    inner = inner_size(parts)
    outer = parts // inner
    chunk = total // parts
    examples = lengths.shape[1]
    count = stored.shape[0]
    wire = jnp.bfloat16 if parts <= 8 else jnp.float32
    vmem = pl.BlockSpec(memory_space=pltpu.VMEM)
    dma = pltpu.SemaphoreType.DMA
    tokens, moved = pl.pallas_call(
        functools.partial(token_kernel, outer, inner),
        out_shape=(
            jax.ShapeDtypeStruct((total, wide), jnp.bfloat16),
            jax.ShapeDtypeStruct((2 * count, rank * rank), jnp.bfloat16),
        ),
        in_specs=[pl.BlockSpec(memory_space=pl.ANY), pl.BlockSpec(memory_space=pl.ANY)] + [vmem] * 5,
        out_specs=(vmem, vmem),
        scratch_shapes=[
            pltpu.VMEM((total, depth_in), jnp.bfloat16),
            pltpu.VMEM((total, depth_out), jnp.bfloat16),
            pltpu.VMEM((wide, depth_in), jnp.bfloat16),
            pltpu.VMEM((wide, depth_out), jnp.bfloat16),
            pltpu.VMEM((outer, chunk, wide), jnp.float32),
            pltpu.VMEM((outer, inner - 1, chunk, wide), wire),
            pltpu.VMEM((outer, inner - 1, chunk, wide), wire),
            pltpu.VMEM((max(outer - 2, 1), chunk, wide), wire),
            pltpu.VMEM((max(outer - 2, 1), chunk, wide), wire),
            pltpu.VMEM((chunk, wide), jnp.float32),
            pltpu.VMEM((chunk, wide), jnp.float32),
            pltpu.VMEM((total, wide), jnp.bfloat16),
            pltpu.VMEM((count * rank, wide), jnp.float32),
            dma((2, parts)),
            dma((outer, inner - 1)), dma((outer, inner - 1)),
            dma((outer - 1,)), dma((outer - 1,)),
            dma((outer - 1,)), dma((outer - 1,)),
            dma((outer, inner - 1)), dma((outer, inner - 1)),
        ],
        compiler_params=pltpu.CompilerParams(
            collective_id=0, has_side_effects=True, vmem_limit_bytes=58 * 1024 * 1024
        ),
    )(layer_inputs, output_grads, proj_in.T, proj_out.T, stored, inv_out, inv_in)
    query = pl.pallas_call(
        sketch_kernel,
        out_shape=jax.ShapeDtypeStruct((2 * examples, rank * rank), jnp.bfloat16),
        in_specs=[vmem, pl.BlockSpec(memory_space=pltpu.SMEM)],
        out_specs=vmem,
        scratch_shapes=[pltpu.VMEM((examples * rank, wide), jnp.float32)],
        compiler_params=pltpu.CompilerParams(vmem_limit_bytes=32 * 1024 * 1024),
    )(tokens, lengths)
    return pl.pallas_call(
        score_kernel,
        out_shape=jax.ShapeDtypeStruct((count, cores * examples), jnp.float32),
        in_specs=[vmem, vmem],
        out_specs=vmem,
        scratch_shapes=[pltpu.VMEM((2 * cores * examples, rank * rank), jnp.bfloat16), dma, dma],
        compiler_params=pltpu.CompilerParams(
            collective_id=1, has_side_effects=True, vmem_limit_bytes=32 * 1024 * 1024
        ),
    )(moved, query)


def solution(mesh):
    placed = (
        P(("groups", "dp"), "tensor"),
        P(("groups", "dp"), "tensor"),
        P("tensor", None),
        P("tensor", None),
        P(),
        P(),
        P(("groups", "tensor", "dp"), None),
        P(("groups", "dp"), None),
    )
    return jax.shard_map(
        functools.partial(on_device, mesh.shape["tensor"], mesh.shape["dp"]),
        mesh=mesh,
        in_specs=placed,
        out_specs=P(("tensor", "dp"), "groups"),
        check_vma=False,
    )
```

```python
import functools
import jax
import jax.numpy as jnp
from jax import lax
from jax.experimental import pallas as pl
from jax.experimental.pallas import tpu as pltpu
from jax.sharding import PartitionSpec as P

MESH = pl.DeviceIdType.MESH
LONGEST = 128
AHEAD = 3
LAG = 1


def window_of(total):
    return min(total, LONGEST + 16)


def inner_size(count):
    inner = 1
    while (2 * inner) ** 3 <= count:
        inner *= 2
    return inner


def flip(place, bits):
    result, bit = place, 1
    while bit <= bits:
        if bits & bit:
            result = result + bit - 2 * bit * ((place // bit) % 2)
        bit *= 2
    return result


def across(left, right):
    return lax.dot_general(left, right, (((1,), (1,)), ((), ())), preferred_element_type=jnp.float32)


def split(value):
    high = value.astype(jnp.bfloat16)
    return high, (value - high.astype(jnp.float32)).astype(jnp.bfloat16)


def move_preconditioner(stored, inv_out, inv_in, mixed, moved):
    count = stored.shape[0]
    rank = inv_in.shape[0]
    wide = 2 * rank
    high, low = split(inv_in[...])
    high = jnp.concatenate([high, high], axis=1)
    low = jnp.concatenate([low, low], axis=1)
    none = jnp.zeros_like(high)
    first = jnp.concatenate([high, none, low, none], axis=0)
    second = jnp.concatenate([none, high, none, low], axis=0)
    for a in range(0, rank, 2):
        pair = stored[:, a * rank:(a + 2) * rank]
        pair = jnp.concatenate([pair, pair], axis=1)
        mixed[pl.ds(a, count, stride=rank), :] = jnp.dot(
            pair, first, preferred_element_type=jnp.float32
        )
        mixed[pl.ds(a + 1, count, stride=rank), :] = jnp.dot(
            pair, second, preferred_element_type=jnp.float32
        )
    out_high, out_low = split(inv_out[...])
    factor = jnp.concatenate([out_high, out_low, out_high], axis=1)

    def one(j, carry):
        rows = pl.ds(pl.multiple_of(j * rank, rank), rank)
        row_high, row_low = split(mixed[rows, :])
        mixed[rows, :] = jnp.dot(
            factor,
            jnp.concatenate([row_high, row_high, row_low], axis=0),
            preferred_element_type=jnp.float32,
        )
        return carry

    lax.fori_loop(0, count, one, 0, unroll=4)
    left = lax.broadcasted_iota(jnp.int32, (count, wide), 1) < rank
    for a in range(0, rank, 2):
        pair = jnp.where(
            left,
            mixed[pl.ds(a, count, stride=rank), :],
            mixed[pl.ds(a + 1, count, stride=rank), :],
        )
        moved[:count, a * rank:(a + 2) * rank], moved[count:, a * rank:(a + 2) * rank] = split(pair)


def token_kernel(
    outer, inner,
    x_hbm, g_hbm, w_in, w_out, stored, inv_out, inv_in,
    tokens_out, moved_out,
    x_buf, g_buf, w_x, w_g, own, send_x, recv_x, send_far, recv_far, send_near, recv_near,
    tokens, mixed,
    load_sem, sx_sem, rx_sem, sz_sem, rz_sem, gz_send, gz_recv, gx_send, gx_recv,
):
    parts = outer * inner
    total = x_buf.shape[0]
    chunk = total // parts
    rank = w_in.shape[0]
    wide = 2 * rank
    me = lax.axis_index("tensor")
    my_o = me // inner
    my_i = me % inner

    def rows_of(o, i):
        return pl.ds(pl.multiple_of((o * inner + i) * chunk, chunk), chunk)

    order = []
    for s in range(outer):
        o = flip(my_o, outer - 1 - s)
        for r in list(range(1, inner)) + [0]:
            order.append((s, r, o, lax.rem(my_i + r, inner)))

    def loads(k):
        _, _, o, i = order[k]
        rows = rows_of(o, i)
        return (
            pltpu.make_async_copy(x_hbm.at[rows], x_buf.at[rows], load_sem.at[0, k]),
            pltpu.make_async_copy(g_hbm.at[rows], g_buf.at[rows], load_sem.at[1, k]),
        )

    for k in range(min(AHEAD, parts)):
        for copy in loads(k):
            copy.start()

    barrier = pltpu.get_barrier_semaphore()
    peers = [{"tensor": flip(my_o, s) * inner + my_i} for s in range(1, outer)]
    peers += [{"tensor": my_o * inner + lax.rem(my_i + r, inner)} for r in range(1, inner)]
    for peer in peers:
        pl.semaphore_signal(barrier, inc=1, device_id=peer, device_id_type=MESH)

    w_x[...] = jnp.concatenate([w_in[...], jnp.zeros_like(w_in)], axis=0)
    w_g[...] = jnp.concatenate([jnp.zeros_like(w_out), w_out[...]], axis=0)
    pl.semaphore_wait(barrier, len(peers))

    sub = min(256, chunk)

    def project(k, dest):
        _, _, o, i = order[k]
        for copy in loads(k):
            copy.wait()
        if k + AHEAD < parts:
            for copy in loads(k + AHEAD):
                copy.start()
        base = (o * inner + i) * chunk

        @pl.loop(0, chunk // sub)
        def _(h):
            rows = pl.ds(pl.multiple_of(base + h * sub, sub), sub)
            value = across(x_buf[rows, :], w_x[...])
            value += across(g_buf[rows, :], w_g[...])
            dest[pl.ds(pl.multiple_of(h * sub, sub), sub), :] = value.astype(dest.dtype)

    def x_copy(s, r):
        return pltpu.make_async_remote_copy(
            src_ref=send_x.at[s, r - 1], dst_ref=recv_x.at[s, r - 1],
            send_sem=sx_sem.at[s, r - 1], recv_sem=rx_sem.at[s, r - 1],
            device_id={"tensor": my_o * inner + lax.rem(my_i + r, inner)}, device_id_type=MESH,
        )

    def send_z(s):
        return send_near if s == outer - 2 else send_far.at[s]

    def recv_z(s):
        return recv_near if s == outer - 2 else recv_far.at[s]

    def z_copy(s):
        return pltpu.make_async_remote_copy(
            src_ref=send_z(s), dst_ref=recv_z(s),
            send_sem=sz_sem.at[s], recv_sem=rz_sem.at[s],
            device_id={"tensor": flip(my_o, outer - 1 - s) * inner + my_i}, device_id_type=MESH,
        )

    def combine(s):
        value = own[s]
        for r in range(1, inner):
            x_copy(s, r).wait_recv()
            value = value + recv_x[s, r - 1].astype(jnp.float32)
        if s < outer - 1:
            target = send_z(s)
            target[...] = value.astype(target.dtype)
            z_copy(s).start()
        else:
            for q in range(outer - 1):
                z_copy(q).wait_recv()
                value = value + recv_z(q)[...].astype(jnp.float32)
            tokens[rows_of(my_o, my_i), :] = value.astype(tokens.dtype)

    for k in range(parts):
        s, r, _, _ = order[k]
        if r:
            project(k, send_x.at[s, r - 1])
            x_copy(s, r).start()
        else:
            project(k, own.at[s])
            if s >= LAG:
                combine(s - LAG)
    for s in range(outer - min(LAG, outer), outer):
        combine(s)

    def gather_z(s):
        rows = rows_of(my_o, my_i)
        return pltpu.make_async_remote_copy(
            src_ref=tokens.at[rows], dst_ref=tokens.at[rows],
            send_sem=gz_send.at[s], recv_sem=gz_recv.at[s],
            device_id={"tensor": flip(my_o, outer - 1 - s) * inner + my_i}, device_id_type=MESH,
        )

    def gather_x(s, r):
        rows = rows_of(flip(my_o, outer - s) if s else my_o, my_i)
        return pltpu.make_async_remote_copy(
            src_ref=tokens.at[rows], dst_ref=tokens.at[rows],
            send_sem=gx_send.at[s, r - 1], recv_sem=gx_recv.at[s, r - 1],
            device_id={"tensor": my_o * inner + lax.rem(my_i + r, inner)}, device_id_type=MESH,
        )

    for s in reversed(range(outer - 1)):
        gather_z(s).start()
    for r in range(1, inner):
        gather_x(0, r).start()
    for s in reversed(range(outer - 1)):
        gather_z(s).wait_recv()
        for r in range(1, inner):
            gather_x(s + 1, r).start()
    move_preconditioner(stored, inv_out, inv_in, mixed, moved_out)
    for s in range(outer):
        for r in range(1, inner):
            gather_x(s, r).wait_recv()

    for s in range(outer):
        for r in range(1, inner):
            x_copy(s, r).wait_send()
            gather_x(s, r).wait_send()
    for s in range(outer - 1):
        z_copy(s).wait_send()
        gather_z(s).wait_send()
    tokens_out[...] = tokens[...]


def sketch_kernel(tokens, lengths, query, sketch):
    total, wide = tokens.shape
    rank = wide // 2
    examples = lengths.shape[1]
    window = window_of(total)
    row = lax.broadcasted_iota(jnp.int32, (window, wide), 0)
    left = lax.broadcasted_iota(jnp.int32, (window, wide), 1) < rank

    def example(e, begin):
        finish = begin + lengths[0, e]
        first = pl.multiple_of(jnp.minimum((begin // 16) * 16, total - window), 16)
        rows = tokens[pl.ds(first, window), :]
        wide_rows = rows.astype(jnp.float32)
        twice = jnp.where(left, wide_rows, pltpu.roll(wide_rows, rank, 1))
        inside = (row >= begin - first) & (row < finish - first)
        picked = jnp.where(inside, twice, 0.0).astype(jnp.bfloat16)
        outer_product = lax.dot_general(
            rows, picked, (((0,), (0,)), ((), ())), preferred_element_type=jnp.float32
        )
        sketch[pl.ds(pl.multiple_of(e * rank, rank), rank), :] = outer_product[rank:, :]
        return finish

    lax.fori_loop(0, examples, example, jnp.int32(0), unroll=8)

    low = lax.broadcasted_iota(jnp.int32, (examples, wide), 1) < rank
    for a in range(0, rank, 2):
        pair = jnp.where(
            low,
            sketch[pl.ds(a, examples, stride=rank), :],
            sketch[pl.ds(a + 1, examples, stride=rank), :],
        )
        columns = slice(a * rank, (a + 2) * rank)
        query[:examples, columns], query[examples:, columns] = split(pair)


def score_kernel(stored, query, out, both, pair_send, pair_recv):
    core = lax.axis_index("dp")
    examples = query.shape[0] // 2
    count = stored.shape[0] // 2
    barrier = pltpu.get_barrier_semaphore()
    pl.semaphore_signal(barrier, inc=1, device_id={"dp": 1 - core}, device_id_type=MESH)
    mine = pl.ds(pl.multiple_of(core * 2 * examples, 2 * examples), 2 * examples)
    both[mine, :] = query[...]
    pl.semaphore_wait(barrier, 1)
    swap = pltpu.make_async_remote_copy(
        src_ref=query, dst_ref=both.at[mine],
        send_sem=pair_send, recv_sem=pair_recv,
        device_id={"dp": 1 - core}, device_id_type=MESH,
    )
    swap.start()
    swap.wait()
    product = across(stored[...], both[...])
    halves = []
    for other in range(both.shape[0] // (2 * examples)):
        at = other * 2 * examples
        high = product[:, at:at + examples]
        halves.append(high[:count] + high[count:] + product[:count, at + examples:at + 2 * examples])
    out[...] = jnp.concatenate(halves, axis=1)


def on_device(parts, cores, layer_inputs, output_grads, proj_in, proj_out, inv_out, inv_in, stored, lengths):
    total, depth_in = layer_inputs.shape
    depth_out = output_grads.shape[1]
    rank = proj_in.shape[1]
    wide = 2 * rank
    inner = inner_size(parts)
    outer = parts // inner
    chunk = total // parts
    examples = lengths.shape[1]
    count = stored.shape[0]
    wire = jnp.bfloat16 if parts <= 8 else jnp.float32
    vmem = pl.BlockSpec(memory_space=pltpu.VMEM)
    dma = pltpu.SemaphoreType.DMA
    tokens, moved = pl.pallas_call(
        functools.partial(token_kernel, outer, inner),
        out_shape=(
            jax.ShapeDtypeStruct((total, wide), jnp.bfloat16),
            jax.ShapeDtypeStruct((2 * count, rank * rank), jnp.bfloat16),
        ),
        in_specs=[pl.BlockSpec(memory_space=pl.ANY), pl.BlockSpec(memory_space=pl.ANY)] + [vmem] * 5,
        out_specs=(vmem, vmem),
        scratch_shapes=[
            pltpu.VMEM((total, depth_in), jnp.bfloat16),
            pltpu.VMEM((total, depth_out), jnp.bfloat16),
            pltpu.VMEM((wide, depth_in), jnp.bfloat16),
            pltpu.VMEM((wide, depth_out), jnp.bfloat16),
            pltpu.VMEM((outer, chunk, wide), jnp.float32),
            pltpu.VMEM((outer, inner - 1, chunk, wide), wire),
            pltpu.VMEM((outer, inner - 1, chunk, wide), wire),
            pltpu.VMEM((max(outer - 2, 1), chunk, wide), wire),
            pltpu.VMEM((max(outer - 2, 1), chunk, wide), wire),
            pltpu.VMEM((chunk, wide), jnp.float32),
            pltpu.VMEM((chunk, wide), jnp.float32),
            pltpu.VMEM((total, wide), jnp.bfloat16),
            pltpu.VMEM((count * rank, wide), jnp.float32),
            dma((2, parts)),
            dma((outer, inner - 1)), dma((outer, inner - 1)),
            dma((outer - 1,)), dma((outer - 1,)),
            dma((outer - 1,)), dma((outer - 1,)),
            dma((outer, inner - 1)), dma((outer, inner - 1)),
        ],
        compiler_params=pltpu.CompilerParams(
            collective_id=0, has_side_effects=True, vmem_limit_bytes=58 * 1024 * 1024
        ),
    )(layer_inputs, output_grads, proj_in.T, proj_out.T, stored, inv_out, inv_in)
    query = pl.pallas_call(
        sketch_kernel,
        out_shape=jax.ShapeDtypeStruct((2 * examples, rank * rank), jnp.bfloat16),
        in_specs=[vmem, pl.BlockSpec(memory_space=pltpu.SMEM)],
        out_specs=vmem,
        scratch_shapes=[pltpu.VMEM((examples * rank, wide), jnp.float32)],
        compiler_params=pltpu.CompilerParams(vmem_limit_bytes=32 * 1024 * 1024),
    )(tokens, lengths)
    return pl.pallas_call(
        score_kernel,
        out_shape=jax.ShapeDtypeStruct((count, cores * examples), jnp.float32),
        in_specs=[vmem, vmem],
        out_specs=vmem,
        scratch_shapes=[pltpu.VMEM((2 * cores * examples, rank * rank), jnp.bfloat16), dma, dma],
        compiler_params=pltpu.CompilerParams(
            collective_id=1, has_side_effects=True, vmem_limit_bytes=32 * 1024 * 1024
        ),
    )(moved, query)


def solution(mesh):
    placed = (
        P(("groups", "dp"), "tensor"),
        P(("groups", "dp"), "tensor"),
        P("tensor", None),
        P("tensor", None),
        P(),
        P(),
        P(("groups", "tensor", "dp"), None),
        P(("groups", "dp"), None),
    )
    return jax.shard_map(
        functools.partial(on_device, mesh.shape["tensor"], mesh.shape["dp"]),
        mesh=mesh,
        in_specs=placed,
        out_specs=P(("tensor", "dp"), "groups"),
        check_vma=False,
    )
```
